32 devices in a mesh: rows: 2 (over core), trans: 8 (over z, x), gvec: 2 (over y).
Axes of the slice: x: 2, y: 2, z: 4, core: 2. Of those that a mesh axis runs over, the one named last changes fastest.
Arguments:
- pair_density: bfloat16 [2, 8192, 4096], P(None, 'trans', 'gvec'), may hold values from -0.75 to 0.75
- coulomb: float32 [4096], P('gvec'), may hold values from 0.1 to 10
- block_index: int32 [2], P('rows'), parts along dimension 0, may hold values from 0 to 7
Outputs:
- kernel_rows: bfloat16 [2, 2048, 8192], P(None, ('rows', 'gvec'), 'trans'), parts along dimension 1
- mirrored: bfloat16 [2, 8192, 2048], P(None, 'trans', 'rows'), parts along dimension 2
The draws below stay inside these ranges and needn't reach their ends.
There are 2 independent parts, one for each index of `rows`. The reference program is written for one: setup_inputs(seed, part) draws one part's arguments, and reference() takes and returns one part's arrays. A program takes and returns all parts, laid end to end along the dimension named above; an argument that names none is the same for every part. Nothing has to cross between parts.
All inputs are finite; a program needn't handle non-finite values.
Results may differ from the reference program's by a relative error of at most 0.017.
Values may be sent and summed in bfloat16 or wider, within the bound.
A program may use at most 64 MiB of HBM per device.

```python
import math
import jax
import jax.numpy as jnp
from jax import lax

NG = 4096
TR_DEV = 1024
NT = 8192
N_TRANS = 8
N_GVEC = 2


def levels(stream_key, extent, split, low, high):
    def one(dim, blocks):
        heights = jax.random.uniform(jax.random.fold_in(jax.random.fold_in(stream_key, 6), dim), (blocks,), jnp.float32, low / len(split), high / len(split))
        return jnp.repeat(jnp.exp(heights), extent[dim] // blocks).reshape((-1,) + (1,) * (len(extent) - dim - 1))

    loudness = one(*split[0])
    for cut in split[1:]:
        loudness = loudness * one(*cut)
    return loudness


def gaussian(stream_key, extent, spread, bound, shards=(), held_as=jnp.bfloat16):
    drawn = spread * jax.random.normal(stream_key, extent, jnp.float32)
    if shards:
        drawn = drawn * levels(stream_key, extent, shards, -0.22, 0.18)
    return jnp.clip(drawn, -bound, bound).astype(held_as)


def setup_inputs(seed: int = 0, part: int = 0) -> dict:
    splits = jax.random.split(jax.random.key(seed), 4)
    own_keys = jax.random.split(jax.random.fold_in(splits[3], part), 4)
    pair_density = gaussian(splits[0], (2, NT, NG), (NG ** -0.25), 0.75, ((1, 8), (2, 2)))
    coulomb = jnp.clip(jnp.exp(math.log(10.0) - 4.6051702 * jax.random.uniform(splits[1], (NG,), jnp.float32) ** levels(splits[1], (NG,), ((0, 2),), -0.2, 0.2)), 0.1, 10.0)
    block_index = jax.random.randint(own_keys[2], (1,), 0, N_TRANS).astype(jnp.int32)
    return {"pair_density": pair_density, "coulomb": coulomb, "block_index": block_index}


def contract(left, right):
    return lax.dot_general(left, right, (((1,), (1,)), ((), ())), precision=lax.Precision.HIGHEST, preferred_element_type=jnp.float32)


def reference(pair_density, coulomb, block_index):
    start = (block_index[0] * TR_DEV).astype(jnp.int32)
    block = lax.dynamic_slice_in_dim(pair_density, start, TR_DEV, 1)
    weighted = (block.astype(jnp.float32) * coulomb[None, None, :]).astype(jnp.bfloat16)
    width = NG // N_GVEC
    real_part = jnp.zeros((TR_DEV, TR_DEV * N_TRANS), jnp.float32)
    imag_part = jnp.zeros((TR_DEV, TR_DEV * N_TRANS), jnp.float32)
    for group in range(N_GVEC):
        low = group * width
        left_real = weighted[0, :, low:low + width].astype(jnp.float32)
        left_imag = weighted[1, :, low:low + width].astype(jnp.float32)
        right_real = pair_density[0, :, low:low + width].astype(jnp.float32)
        right_imag = pair_density[1, :, low:low + width].astype(jnp.float32)
        term_real = (contract(left_real, right_real) + contract(left_imag, right_imag)).astype(jnp.bfloat16)
        term_imag = (contract(left_real, right_imag) - contract(left_imag, right_real)).astype(jnp.bfloat16)
        term_real, term_imag = lax.optimization_barrier((term_real, term_imag))
        real_part = real_part + term_real.astype(jnp.float32)
        imag_part = imag_part + term_imag.astype(jnp.float32)
    real_out = real_part.astype(jnp.bfloat16)
    imag_out = imag_part.astype(jnp.bfloat16)
    kernel_rows = jnp.stack([real_out, imag_out])
    mirrored = jnp.stack([real_out.T, -imag_out.T])
    return kernel_rows, mirrored
```

```python
import functools

import jax
import jax.numpy as jnp
from jax import lax
from jax.experimental import pallas as pl
from jax.experimental.pallas import tpu as pltpu
from jax.sharding import PartitionSpec as P

MESH = pl.DeviceIdType.MESH
CHUNK = 32
GROUP = 128
HOP = 2
OTHER = 4
SETTLE = 2


def contract(left, right):
    return lax.dot_general(
        left, right, (((1,), (1,)), ((), ())), preferred_element_type=jnp.float32
    )


def kernel(
    n, ng, index_ref, pd_ref, coulomb_ref, rows_ref, mirror_ref,
    near, up, down, final, other, weighted, weighted_other, term, arrived,
    near_send, near_recv, share_send, share_recv, up_send, up_recv,
    down_send, down_recv, cross_send, cross_recv, term_send, term_recv,
):
    r, t, y = lax.axis_index("rows"), lax.axis_index("trans"), lax.axis_index("gvec")
    line = n // 2
    z, x = t // 2, t % 2
    chunks = near.shape[0]
    half = chunks * CHUNK
    groups = term.shape[0]
    depth = pd_ref.shape[2]
    per = GROUP // CHUNK
    tiles = pd_ref.shape[1]
    across = {"trans": 2 * z + 1 - x}
    above, below = {"trans": t + 2}, {"trans": t - 2}
    sibling = {"rows": 1 - r}

    barrier = pltpu.get_barrier_semaphore()

    def greet(device):
        pl.semaphore_signal(barrier, inc=1, device_id=device, device_id_type=MESH)

    greet(across)
    greet(sibling)
    for p in range(1, ng):
        greet({"gvec": (y + p) % ng})

    @pl.when(z > 0)
    def _():
        greet(below)

    @pl.when(z < line - 1)
    def _():
        greet(above)

    pl.semaphore_wait(
        barrier, 1 + ng + jnp.where(z > 0, 1, 0) + jnp.where(z < line - 1, 1, 0)
    )

    def remote(source, target, send, recv, device):
        return pltpu.make_async_remote_copy(
            src_ref=source, dst_ref=target, send_sem=send, recv_sem=recv,
            device_id=device, device_id_type=MESH,
        )

    def own_rows(side, c):
        return pl.ds(pl.multiple_of(side * half + c * CHUNK, CHUNK), CHUNK)

    def near_copy(c):
        return remote(
            pd_ref.at[r, own_rows(1 - x, c), :], near.at[c, r],
            near_send.at[c], near_recv.at[c], across,
        )

    def share_copy(c):
        return remote(near.at[c, r], near.at[c, r], share_send.at[c], share_recv.at[c], sibling)

    def up_copy(c):
        return remote(up.at[c], up.at[c], up_send.at[c], up_recv.at[c], above)

    def down_copy(c):
        return remote(down.at[c], down.at[c], down_send.at[c], down_recv.at[c], below)

    def cross_copy(c):
        return remote(final.at[c], other.at[c], cross_send.at[c], cross_recv.at[c], across)

    def term_copy(g, p):
        return remote(
            term.at[g], arrived.at[p - 1, g], term_send.at[p - 1, g], term_recv.at[p - 1, g],
            {"gvec": (y + p) % ng},
        )

    source = index_ref[0]
    source_z, source_x = source // 2, source % 2
    here = source_z == z
    mine = source_x == x

    def start_near(c, carry):
        near_copy(c).start()
        return carry

    lax.fori_loop(0, chunks, start_near, 0)
    near_copy(0).wait_recv()
    share_copy(0).start()

    def base(c):
        return jnp.where(mine, pd_ref[:, own_rows(x, c), :], near[c])

    def weigh(held, c, target):
        at = pl.multiple_of((c % per) * CHUNK, CHUNK)
        scale = coulomb_ref[...]
        real = (held[0].astype(jnp.float32) * scale).astype(jnp.bfloat16)
        imag = (held[1].astype(jnp.float32) * scale).astype(jnp.bfloat16)
        target[pl.ds(at, CHUNK), :depth] = real
        target[pl.ds(at, CHUNK), depth:] = imag
        target[pl.ds(GROUP + at, CHUNK), :depth] = -imag
        target[pl.ds(GROUP + at, CHUNK), depth:] = real

    def multiply(g, target):
        tile = min(512, tiles)

        def one(i, carry):
            at = pl.ds(pl.multiple_of(i * tile, tile), tile)
            total = contract(pd_ref[0, at, :], target[:, :depth])
            total = total + contract(pd_ref[1, at, :], target[:, depth:])
            term[g, at, :] = total.astype(jnp.bfloat16)
            return carry

        lax.fori_loop(0, tiles // tile, one, 0)
        for p in range(1, ng):
            term_copy(g, p).start()

    def settle(g):
        for p in range(1, ng):
            term_copy(g, p).wait_recv()
        tile = min(256, tiles)

        def one(i, carry):
            at = pl.ds(pl.multiple_of(i * tile, tile), tile)
            total = term[g, at, :].astype(jnp.float32)
            for p in range(1, ng):
                total = total + arrived[p - 1, g, at, :].astype(jnp.float32)
            columns = pl.ds(pl.multiple_of(g * GROUP, GROUP), GROUP)
            summed = total.astype(jnp.bfloat16)
            mirror_ref[0, at, columns] = summed[:, :GROUP]
            mirror_ref[1, at, columns] = -summed[:, GROUP:]

            @pl.when(g // (groups // ng) == y)
            def _():
                to = pl.ds(pl.multiple_of((g % (groups // ng)) * GROUP, GROUP), GROUP)
                rows_ref[0, to, at] = summed[:, :GROUP].T
                rows_ref[1, to, at] = summed[:, GROUP:].T

            return carry

        lax.fori_loop(0, tiles // tile, one, 0)

    side_groups = groups // 2
    lag = (line - 1) * HOP

    def step(s, carry):
        @pl.when(s + 1 < chunks)
        def _():
            near_copy(s + 1).wait_recv()
            share_copy(s + 1).start()

        @pl.when(s < chunks)
        def _():
            share_copy(s).wait_recv()

        u = s - z * HOP

        @pl.when((u >= 0) & (u < chunks))
        def _():
            @pl.when(z == 0)
            def _():
                up[u] = base(u)

            @pl.when(z > 0)
            def _():
                up_copy(u).wait_recv()
                up[u] = jnp.where(here, base(u), up[u])

            @pl.when(z < line - 1)
            def _():
                up_copy(u).start()

        d = s - (line - 1 - z) * HOP

        @pl.when((d >= 0) & (d < chunks))
        def _():
            @pl.when(z == line - 1)
            def _():
                down[d] = base(d)

            @pl.when(z < line - 1)
            def _():
                down_copy(d).wait_recv()
                down[d] = jnp.where(here, base(d), down[d])

            @pl.when(z > 0)
            def _():
                down_copy(d).start()

        f = s - lag

        @pl.when((f >= 0) & (f < chunks))
        def _():
            final[f] = jnp.where(source_z <= z, up[f], down[f])
            cross_copy(f).start()
            weigh(final[f], f, weighted)

            @pl.when(f % per == per - 1)
            def _():
                multiply(x * side_groups + f // per, weighted)

        o = f - OTHER

        @pl.when((o >= 0) & (o < chunks))
        def _():
            cross_copy(o).wait_recv()
            weigh(other[o], o, weighted_other)

            @pl.when(o % per == per - 1)
            def _():
                multiply((1 - x) * side_groups + o // per, weighted_other)

        a = f - SETTLE

        @pl.when((a >= 0) & (a < chunks) & (a % per == per - 1))
        def _():
            settle(x * side_groups + a // per)

        b = o - SETTLE

        @pl.when((b >= 0) & (b < chunks) & (b % per == per - 1))
        def _():
            settle((1 - x) * side_groups + b // per)

        return carry

    lax.fori_loop(0, chunks + lag + OTHER + SETTLE, step, 0)

    def drain(c, carry):
        near_copy(c).wait_send()
        share_copy(c).wait_send()
        cross_copy(c).wait_send()

        @pl.when(z < line - 1)
        def _():
            up_copy(c).wait_send()

        @pl.when(z > 0)
        def _():
            down_copy(c).wait_send()

        return carry

    lax.fori_loop(0, chunks, drain, 0)

    def drain_terms(g, carry):
        for p in range(1, ng):
            term_copy(g, p).wait_send()
        return carry

    lax.fori_loop(0, groups, drain_terms, 0)


def solution(mesh):
    n, ng = mesh.shape["trans"], mesh.shape["gvec"]

    def body(pair_density, coulomb, block_index):
        _, rows, depth = pair_density.shape
        chunks = rows // 2 // CHUNK
        groups = rows // GROUP
        slots = pltpu.VMEM((chunks, 2, CHUNK, depth), jnp.bfloat16)
        sems = pltpu.SemaphoreType.DMA((chunks,))
        vmem = pl.BlockSpec(memory_space=pltpu.VMEM)
        return pl.pallas_call(
            functools.partial(kernel, n, ng),
            out_shape=(
                jax.ShapeDtypeStruct((2, rows // ng, rows), jnp.bfloat16),
                jax.ShapeDtypeStruct((2, rows, rows), jnp.bfloat16),
            ),
            in_specs=[pl.BlockSpec(memory_space=pltpu.SMEM), vmem, vmem],
            out_specs=(vmem, vmem),
            scratch_shapes=[slots] * 5
            + [pltpu.VMEM((2 * GROUP, 2 * depth), jnp.bfloat16)] * 2
            + [
                pltpu.VMEM((groups, rows, 2 * GROUP), jnp.bfloat16),
                pltpu.VMEM((ng - 1, groups, rows, 2 * GROUP), jnp.bfloat16),
            ]
            + [sems] * 10
            + [pltpu.SemaphoreType.DMA((ng - 1, groups))] * 2,
            compiler_params=pltpu.CompilerParams(
                collective_id=0, has_side_effects=True, vmem_limit_bytes=58 * 2**20
            ),
            cost_estimate=pl.CostEstimate(
                flops=8 * rows * rows * depth, bytes_accessed=28 * 2**20, transcendentals=0
            ),
        )(block_index, pair_density, coulomb[None, :])

    placed = (P(None, "trans", "gvec"), P("gvec"), P("rows"))
    return jax.shard_map(
        body,
        mesh=mesh,
        in_specs=placed,
        out_specs=(P(None, ("rows", "gvec"), "trans"), P(None, "trans", "rows")),
        check_vma=False,
    )
```

```python
import functools

import jax
import jax.numpy as jnp
from jax import lax
from jax.experimental import pallas as pl
from jax.experimental.pallas import tpu as pltpu
from jax.sharding import PartitionSpec as P

MESH = pl.DeviceIdType.MESH
CHUNK = 16
GROUP = 128
PART = 64
HOP = 2
OTHER = 12
SETTLE = 3


def contract(left, right):
    return lax.dot_general(
        left, right, (((1,), (1,)), ((), ())), preferred_element_type=jnp.float32
    )


def kernel(
    n, ng, index_ref, pd_in, coulomb_ref, rows_out, mirror_out,
    pd_ref, rows_ref, mirror_ref, near, up, down, final, other, weighted, weighted_other, term, arrived,
    near_send, near_recv, share_send, share_recv, up_send, up_recv,
    down_send, down_recv, cross_send, cross_recv, term_send, term_recv,
    load_sem, rows_sem, mirror_sem,
):
    r, t, y = lax.axis_index("rows"), lax.axis_index("trans"), lax.axis_index("gvec")
    line = n // 2
    z, x = t // 2, t % 2
    chunks = near.shape[0]
    half = chunks * CHUNK
    groups = term.shape[0]
    depth = pd_ref.shape[2]
    per = GROUP // CHUNK
    tiles = pd_ref.shape[1]
    across = {"trans": 2 * z + 1 - x}
    above, below = {"trans": t + 2}, {"trans": t - 2}
    sibling = {"rows": 1 - r}
    load = pltpu.make_async_copy(pd_in, pd_ref, load_sem)
    load.start()

    barrier = pltpu.get_barrier_semaphore()

    def greet(device):
        pl.semaphore_signal(barrier, inc=1, device_id=device, device_id_type=MESH)

    greet(across)
    greet(sibling)
    for p in range(1, ng):
        greet({"gvec": (y + p) % ng})

    @pl.when(z > 0)
    def _():
        greet(below)

    @pl.when(z < line - 1)
    def _():
        greet(above)

    pl.semaphore_wait(
        barrier, 1 + ng + jnp.where(z > 0, 1, 0) + jnp.where(z < line - 1, 1, 0)
    )

    def remote(source, target, send, recv, device):
        return pltpu.make_async_remote_copy(
            src_ref=source, dst_ref=target, send_sem=send, recv_sem=recv,
            device_id=device, device_id_type=MESH,
        )

    def own_rows(side, c):
        return pl.ds(pl.multiple_of(side * half + c * CHUNK, CHUNK), CHUNK)

    def near_copy(c):
        return remote(
            pd_in.at[r, own_rows(1 - x, c), :], near.at[c, r],
            near_send.at[c], near_recv.at[c], across,
        )

    def share_copy(c):
        return remote(near.at[c, r], near.at[c, r], share_send.at[c], share_recv.at[c], sibling)

    def up_copy(c):
        return remote(up.at[c], up.at[c], up_send.at[c], up_recv.at[c], above)

    def down_copy(c):
        return remote(down.at[c], down.at[c], down_send.at[c], down_recv.at[c], below)

    def cross_copy(c):
        return remote(final.at[c], other.at[c], cross_send.at[c], cross_recv.at[c], across)

    def term_copy(g, part, p):
        wide = pl.ds(pl.multiple_of(part * 2 * PART, 2 * PART), 2 * PART)
        return remote(
            term.at[g, :, wide], arrived.at[p - 1, g, :, wide],
            term_send.at[p - 1, g, part], term_recv.at[p - 1, g, part],
            {"gvec": (y + p) % ng},
        )

    def columns(g):
        return pl.ds(pl.multiple_of(g * GROUP, GROUP), GROUP)

    def mirror_copy(g):
        return pltpu.make_async_copy(
            mirror_ref.at[:, :, columns(g)], mirror_out.at[:, :, columns(g)], mirror_sem.at[g]
        )

    def rows_copy(g):
        return pltpu.make_async_copy(
            rows_ref.at[:, columns(g), :], rows_out.at[:, columns(g), :], rows_sem.at[g]
        )

    source = index_ref[0]
    source_z, source_x = source // 2, source % 2
    here = source_z == z
    mine = source_x == x

    def start_near(c, carry):
        near_copy(c).start()
        return carry

    lax.fori_loop(0, chunks, start_near, 0)
    load.wait()
    near_copy(0).wait_recv()
    share_copy(0).start()

    def base(c):
        return jnp.where(mine, pd_ref[:, own_rows(x, c), :], near[c])

    def weigh(held, c, target):
        row = (c % per) * CHUNK
        at = pl.multiple_of((row // PART) * 2 * PART + row % PART, CHUNK)
        scale = coulomb_ref[...]
        real = (held[0].astype(jnp.float32) * scale).astype(jnp.bfloat16)
        imag = (held[1].astype(jnp.float32) * scale).astype(jnp.bfloat16)
        target[pl.ds(at, CHUNK), :depth] = real
        target[pl.ds(at, CHUNK), depth:] = imag
        target[pl.ds(PART + at, CHUNK), :depth] = -imag
        target[pl.ds(PART + at, CHUNK), depth:] = real

    def multiply(g, parts, target):
        tile = min(512, tiles)
        lanes = 2 * PART * len(parts)
        first = parts[0] * 2 * PART

        def one(i, carry):
            at = pl.ds(pl.multiple_of(i * tile, tile), tile)
            total = contract(pd_ref[0, at, :], target[first:first + lanes, :depth])
            total = total + contract(pd_ref[1, at, :], target[first:first + lanes, depth:])
            term[g, at, first:first + lanes] = total.astype(jnp.bfloat16)
            return carry

        lax.fori_loop(0, tiles // tile, one, 0)
        for part in parts:
            for p in range(1, ng):
                term_copy(g, part, p).start()

    def settle(g):
        for part in range(GROUP // PART):
            for p in range(1, ng):
                term_copy(g, part, p).wait_recv()
        tile = min(256, tiles)
        share = groups // ng

        def one(i, carry):
            at = pl.ds(pl.multiple_of(i * tile, tile), tile)
            total = term[g, at, :].astype(jnp.float32)
            for p in range(1, ng):
                total = total + arrived[p - 1, g, at, :].astype(jnp.float32)
            summed = total.astype(jnp.bfloat16)
            real = jnp.concatenate([summed[:, :PART], summed[:, 2 * PART:3 * PART]], axis=1)
            imag = jnp.concatenate([summed[:, PART:2 * PART], summed[:, 3 * PART:]], axis=1)
            mirror_ref[0, at, columns(g)] = real
            mirror_ref[1, at, columns(g)] = -imag

            @pl.when(g // share == y)
            def _():
                rows_ref[0, columns(g % share), at] = real.T
                rows_ref[1, columns(g % share), at] = imag.T

            return carry

        lax.fori_loop(0, tiles // tile, one, 0)
        mirror_copy(g).start()

        @pl.when(g // share == y)
        def _():
            rows_copy(g % share).start()

    side_groups = groups // 2
    lag = (line - 1) * HOP

    def step(s, carry):
        @pl.when(s + 1 < chunks)
        def _():
            near_copy(s + 1).wait_recv()
            share_copy(s + 1).start()

        @pl.when(s < chunks)
        def _():
            share_copy(s).wait_recv()

        u = s - z * HOP

        @pl.when((u >= 0) & (u < chunks))
        def _():
            @pl.when(z == 0)
            def _():
                up[u] = base(u)

            @pl.when(z > 0)
            def _():
                up_copy(u).wait_recv()
                up[u] = jnp.where(here, base(u), up[u])

            @pl.when(z < line - 1)
            def _():
                up_copy(u).start()

        d = s - (line - 1 - z) * HOP

        @pl.when((d >= 0) & (d < chunks))
        def _():
            @pl.when(z == line - 1)
            def _():
                down[d] = base(d)

            @pl.when(z < line - 1)
            def _():
                down_copy(d).wait_recv()
                down[d] = jnp.where(here, base(d), down[d])

            @pl.when(z > 0)
            def _():
                down_copy(d).start()

        f = s - lag

        @pl.when((f >= 0) & (f < chunks))
        def _():
            final[f] = jnp.where(source_z <= z, up[f], down[f])
            cross_copy(f).start()
            weigh(final[f], f, weighted)

            @pl.when(f % per == per - 1)
            def _():
                multiply(x * side_groups + f // per, (0, 1), weighted)

        o = f - OTHER

        @pl.when((o >= 0) & (o < chunks))
        def _():
            cross_copy(o).wait_recv()
            weigh(other[o], o, weighted_other)

            for part in range(GROUP // PART):
                @pl.when(o % per == (part + 1) * (PART // CHUNK) - 1)
                def _(part=part):
                    multiply((1 - x) * side_groups + o // per, (part,), weighted_other)

        a = f - SETTLE

        @pl.when((a >= 0) & (a < chunks) & (a % per == per - 1))
        def _():
            settle(x * side_groups + a // per)

        b = o - SETTLE

        @pl.when((b >= 0) & (b < chunks) & (b % per == per - 1))
        def _():
            settle((1 - x) * side_groups + b // per)

        return carry

    lax.fori_loop(0, chunks + lag + OTHER + SETTLE, step, 0)

    def drain(c, carry):
        near_copy(c).wait_send()
        share_copy(c).wait_send()
        cross_copy(c).wait_send()

        @pl.when(z < line - 1)
        def _():
            up_copy(c).wait_send()

        @pl.when(z > 0)
        def _():
            down_copy(c).wait_send()

        return carry

    lax.fori_loop(0, chunks, drain, 0)

    def drain_terms(g, carry):
        for part in range(GROUP // PART):
            for p in range(1, ng):
                term_copy(g, part, p).wait_send()
        mirror_copy(g).wait()
        return carry

    lax.fori_loop(0, groups, drain_terms, 0)

    def drain_rows(g, carry):
        rows_copy(g).wait()
        return carry

    lax.fori_loop(0, groups // ng, drain_rows, 0)


def solution(mesh):
    n, ng = mesh.shape["trans"], mesh.shape["gvec"]

    def body(pair_density, coulomb, block_index):
        _, rows, depth = pair_density.shape
        chunks = rows // 2 // CHUNK
        groups = rows // GROUP
        slots = pltpu.VMEM((chunks, 2, CHUNK, depth), jnp.bfloat16)
        sems = pltpu.SemaphoreType.DMA((chunks,))
        vmem = pl.BlockSpec(memory_space=pltpu.VMEM)
        hbm = pl.BlockSpec(memory_space=pl.ANY)
        return pl.pallas_call(
            functools.partial(kernel, n, ng),
            out_shape=(
                jax.ShapeDtypeStruct((2, rows // ng, rows), jnp.bfloat16),
                jax.ShapeDtypeStruct((2, rows, rows), jnp.bfloat16),
            ),
            in_specs=[pl.BlockSpec(memory_space=pltpu.SMEM), hbm, vmem],
            out_specs=(hbm, hbm),
            scratch_shapes=[
                pltpu.VMEM(pair_density.shape, jnp.bfloat16),
                pltpu.VMEM((2, rows // ng, rows), jnp.bfloat16),
                pltpu.VMEM((2, rows, rows), jnp.bfloat16),
            ]
            + [slots] * 5
            + [pltpu.VMEM((2 * GROUP, 2 * depth), jnp.bfloat16)] * 2
            + [
                pltpu.VMEM((groups, rows, 2 * GROUP), jnp.bfloat16),
                pltpu.VMEM((ng - 1, groups, rows, 2 * GROUP), jnp.bfloat16),
            ]
            + [sems] * 10
            + [pltpu.SemaphoreType.DMA((ng - 1, groups, GROUP // PART))] * 2
            + [
                pltpu.SemaphoreType.DMA,
                pltpu.SemaphoreType.DMA((groups // ng,)),
                pltpu.SemaphoreType.DMA((groups,)),
            ],
            compiler_params=pltpu.CompilerParams(
                collective_id=0, has_side_effects=True, vmem_limit_bytes=58 * 2**20
            ),
            cost_estimate=pl.CostEstimate(
                flops=8 * rows * rows * depth, bytes_accessed=28 * 2**20, transcendentals=0
            ),
        )(block_index, pair_density, coulomb[None, :])

    placed = (P(None, "trans", "gvec"), P("gvec"), P("rows"))
    return jax.shard_map(
        body,
        mesh=mesh,
        in_specs=placed,
        out_specs=(P(None, ("rows", "gvec"), "trans"), P(None, "trans", "rows")),
        check_vma=False,
    )
```

```python
import functools

import jax
import jax.numpy as jnp
from jax import lax
from jax.experimental import pallas as pl
from jax.experimental.pallas import tpu as pltpu
from jax.sharding import PartitionSpec as P

MESH = pl.DeviceIdType.MESH
CHUNK = 16
GROUP = 128
PART = 64
HOP = 2
OTHER = 12
SETTLE = 3
TILE = 256


def contract(left, right):
    return lax.dot_general(
        left, right, (((1,), (1,)), ((), ())), preferred_element_type=jnp.float32
    )


def kernel(
    n, ng, index_ref, pd_in, coulomb_ref, rows_out, mirror_out,
    pd_ref, rows_ref, mirror_ref, near, up, down, final, other, weighted, weighted_other, term, arrived,
    near_send, near_recv, share_send, share_recv, up_send, up_recv,
    down_send, down_recv, cross_send, cross_recv, term_send, term_recv,
    load_sem, rows_sem, mirror_sem,
):
    r, t, y = lax.axis_index("rows"), lax.axis_index("trans"), lax.axis_index("gvec")
    line = n // 2
    z, x = t // 2, t % 2
    chunks = near.shape[0]
    half = chunks * CHUNK
    groups = term.shape[0]
    depth = pd_ref.shape[2]
    per = GROUP // CHUNK
    tiles = pd_ref.shape[1] // TILE
    across = {"trans": 2 * z + 1 - x}
    above, below = {"trans": t + 2}, {"trans": t - 2}
    sibling = {"rows": 1 - r}
    load = pltpu.make_async_copy(pd_in, pd_ref, load_sem)
    load.start()

    barrier = pltpu.get_barrier_semaphore()

    def greet(device):
        pl.semaphore_signal(barrier, inc=1, device_id=device, device_id_type=MESH)

    greet(across)
    greet(sibling)
    for p in range(1, ng):
        greet({"gvec": (y + p) % ng})

    @pl.when(z > 0)
    def _():
        greet(below)

    @pl.when(z < line - 1)
    def _():
        greet(above)

    pl.semaphore_wait(
        barrier, 1 + ng + jnp.where(z > 0, 1, 0) + jnp.where(z < line - 1, 1, 0)
    )

    def remote(source, target, send, recv, device):
        return pltpu.make_async_remote_copy(
            src_ref=source, dst_ref=target, send_sem=send, recv_sem=recv,
            device_id=device, device_id_type=MESH,
        )

    def own_rows(side, c):
        return pl.ds(pl.multiple_of(side * half + c * CHUNK, CHUNK), CHUNK)

    def near_copy(c):
        return remote(
            pd_in.at[r, own_rows(1 - x, c), :], near.at[c, r],
            near_send.at[c], near_recv.at[c], across,
        )

    def share_copy(c):
        return remote(near.at[c, r], near.at[c, r], share_send.at[c], share_recv.at[c], sibling)

    def up_copy(c):
        return remote(up.at[c], up.at[c], up_send.at[c], up_recv.at[c], above)

    def down_copy(c):
        return remote(down.at[c], down.at[c], down_send.at[c], down_recv.at[c], below)

    def cross_copy(c):
        return remote(final.at[c], other.at[c], cross_send.at[c], cross_recv.at[c], across)

    def rows_of(i):
        return pl.ds(pl.multiple_of(i * TILE, TILE), TILE)

    def term_copy(g, i, part, p):
        if part is None:
            lanes, slot = pl.ds(0, 2 * GROUP), 0
        else:
            lanes, slot = pl.ds(pl.multiple_of(part * 2 * PART, 2 * PART), 2 * PART), part
        return remote(
            term.at[g, rows_of(i), lanes], arrived.at[p - 1, g, rows_of(i), lanes],
            term_send.at[p - 1, g, i, slot], term_recv.at[p - 1, g, i, slot],
            {"gvec": (y + p) % ng},
        )

    def columns(g):
        return pl.ds(pl.multiple_of(g * GROUP, GROUP), GROUP)

    def mirror_copy(g):
        return pltpu.make_async_copy(
            mirror_ref.at[:, :, columns(g)], mirror_out.at[:, :, columns(g)], mirror_sem.at[g]
        )

    def rows_copy(g):
        return pltpu.make_async_copy(
            rows_ref.at[:, columns(g), :], rows_out.at[:, columns(g), :], rows_sem.at[g]
        )

    source = index_ref[0]
    source_z, source_x = source // 2, source % 2
    here = source_z == z
    mine = source_x == x

    def start_near(c, carry):
        near_copy(c).start()
        return carry

    lax.fori_loop(0, chunks, start_near, 0)
    load.wait()
    near_copy(0).wait_recv()
    share_copy(0).start()

    def base(c):
        return jnp.where(mine, pd_ref[:, own_rows(x, c), :], near[c])

    def weigh(held, row, slot, target):
        at = pl.multiple_of((row // PART) * 2 * PART + row % PART, CHUNK)
        scale = coulomb_ref[...]
        real = (held[0].astype(jnp.float32) * scale).astype(jnp.bfloat16)
        imag = (held[1].astype(jnp.float32) * scale).astype(jnp.bfloat16)
        target[slot, pl.ds(at, CHUNK), :depth] = real
        target[slot, pl.ds(at, CHUNK), depth:] = imag
        target[slot, pl.ds(PART + at, CHUNK), :depth] = -imag
        target[slot, pl.ds(PART + at, CHUNK), depth:] = real

    def multiply(i, left):
        total = contract(pd_ref[0, rows_of(i), :], left[:, :depth])
        total = total + contract(pd_ref[1, rows_of(i), :], left[:, depth:])
        return total.astype(jnp.bfloat16)

    share = groups // ng

    def settle(g, i, parts):
        for part in parts:
            for p in range(1, ng):
                term_copy(g, i, part, p).wait_recv()
        at = rows_of(i)
        total = term[g, at, :].astype(jnp.float32)
        for p in range(1, ng):
            total = total + arrived[p - 1, g, at, :].astype(jnp.float32)
        summed = total.astype(jnp.bfloat16)
        real = jnp.concatenate([summed[:, :PART], summed[:, 2 * PART:3 * PART]], axis=1)
        imag = jnp.concatenate([summed[:, PART:2 * PART], summed[:, 3 * PART:]], axis=1)
        mirror_ref[0, at, columns(g)] = real
        mirror_ref[1, at, columns(g)] = -imag

        @pl.when(g // share == y)
        def _():
            rows_ref[0, columns(g % share), at] = real.T
            rows_ref[1, columns(g % share), at] = imag.T

        @pl.when(i == tiles - 1)
        def _():
            mirror_copy(g).start()

            @pl.when(g // share == y)
            def _():
                rows_copy(g % share).start()

    side_groups = groups // 2
    lag = (line - 1) * HOP
    per_part = PART // CHUNK
    pace = per // tiles
    assert per_part == tiles and pace == 2

    def step(s, carry):
        @pl.when(s + 1 < chunks)
        def _():
            near_copy(s + 1).wait_recv()
            share_copy(s + 1).start()

        @pl.when(s < chunks)
        def _():
            share_copy(s).wait_recv()

        u = s - z * HOP

        @pl.when((u >= 0) & (u < chunks))
        def _():
            @pl.when(z == 0)
            def _():
                up[u] = base(u)

            @pl.when(z > 0)
            def _():
                up_copy(u).wait_recv()
                up[u] = jnp.where(here, base(u), up[u])

            @pl.when(z < line - 1)
            def _():
                up_copy(u).start()

        d = s - (line - 1 - z) * HOP

        @pl.when((d >= 0) & (d < chunks))
        def _():
            @pl.when(z == line - 1)
            def _():
                down[d] = base(d)

            @pl.when(z < line - 1)
            def _():
                down_copy(d).wait_recv()
                down[d] = jnp.where(here, base(d), down[d])

            @pl.when(z > 0)
            def _():
                down_copy(d).start()

        f = s - lag

        @pl.when((f >= 0) & (f < chunks))
        def _():
            final[f] = jnp.where(source_z <= z, up[f], down[f])
            cross_copy(f).start()
            weigh(final[f], (f % per) * CHUNK, (f // per) % 2, weighted)

        o = f - OTHER

        @pl.when((o >= 0) & (o < chunks))
        def _():
            cross_copy(o).wait_recv()
            weigh(other[o], (o % per_part) * CHUNK, (o // per_part) % 2, weighted_other)

        m = f - per

        @pl.when((m >= 0) & (m < chunks) & (m % pace == 0))
        def _():
            q, i = m // per, (m % per) // pace
            g = x * side_groups + q
            term[g, rows_of(i), :] = multiply(i, weighted.at[q % 2])
            for p in range(1, ng):
                term_copy(g, i, None, p).start()

        m = o - per_part

        @pl.when((m >= 0) & (m < chunks))
        def _():
            q, i = m // per_part, m % per_part
            g = (1 - x) * side_groups + q // 2
            for part in range(2):
                @pl.when(q % 2 == part)
                def _(part=part):
                    term[g, rows_of(i), part * 2 * PART:(part + 1) * 2 * PART] = multiply(
                        i, weighted_other.at[part]
                    )
                    for p in range(1, ng):
                        term_copy(g, i, part, p).start()

        a = f - per - SETTLE

        @pl.when((a >= 0) & (a < chunks) & (a % pace == 0))
        def _():
            settle(x * side_groups + a // per, (a % per) // pace, (None,))

        b = o - per - SETTLE

        @pl.when((b >= 0) & (b < chunks) & (b % per < tiles))
        def _():
            settle((1 - x) * side_groups + b // per, b % per, (0, 1))

        return carry

    lax.fori_loop(0, chunks + lag + OTHER + per + SETTLE, step, 0)

    def drain(c, carry):
        near_copy(c).wait_send()
        share_copy(c).wait_send()
        cross_copy(c).wait_send()

        @pl.when(z < line - 1)
        def _():
            up_copy(c).wait_send()

        @pl.when(z > 0)
        def _():
            down_copy(c).wait_send()

        return carry

    lax.fori_loop(0, chunks, drain, 0)

    def drain_terms(g, carry):
        def drain_tile(i, inner):
            for p in range(1, ng):
                term_copy(x * side_groups + g, i, None, p).wait_send()
                for part in range(2):
                    term_copy((1 - x) * side_groups + g, i, part, p).wait_send()
            return inner

        lax.fori_loop(0, tiles, drain_tile, 0)
        mirror_copy(g).wait()
        mirror_copy(side_groups + g).wait()
        return carry

    lax.fori_loop(0, side_groups, drain_terms, 0)

    def drain_rows(g, carry):
        rows_copy(g).wait()
        return carry

    lax.fori_loop(0, groups // ng, drain_rows, 0)


def solution(mesh):
    n, ng = mesh.shape["trans"], mesh.shape["gvec"]

    def body(pair_density, coulomb, block_index):
        _, rows, depth = pair_density.shape
        chunks = rows // 2 // CHUNK
        groups = rows // GROUP
        slots = pltpu.VMEM((chunks, 2, CHUNK, depth), jnp.bfloat16)
        sems = pltpu.SemaphoreType.DMA((chunks,))
        vmem = pl.BlockSpec(memory_space=pltpu.VMEM)
        hbm = pl.BlockSpec(memory_space=pl.ANY)
        return pl.pallas_call(
            functools.partial(kernel, n, ng),
            out_shape=(
                jax.ShapeDtypeStruct((2, rows // ng, rows), jnp.bfloat16),
                jax.ShapeDtypeStruct((2, rows, rows), jnp.bfloat16),
            ),
            in_specs=[pl.BlockSpec(memory_space=pltpu.SMEM), hbm, vmem],
            out_specs=(hbm, hbm),
            scratch_shapes=[
                pltpu.VMEM(pair_density.shape, jnp.bfloat16),
                pltpu.VMEM((2, rows // ng, rows), jnp.bfloat16),
                pltpu.VMEM((2, rows, rows), jnp.bfloat16),
            ]
            + [slots] * 5
            + [
                pltpu.VMEM((2, 2 * GROUP, 2 * depth), jnp.bfloat16),
                pltpu.VMEM((2, 2 * PART, 2 * depth), jnp.bfloat16),
            ]
            + [
                pltpu.VMEM((groups, rows, 2 * GROUP), jnp.bfloat16),
                pltpu.VMEM((ng - 1, groups, rows, 2 * GROUP), jnp.bfloat16),
            ]
            + [sems] * 10
            + [pltpu.SemaphoreType.DMA((ng - 1, groups, rows // TILE, GROUP // PART))] * 2
            + [
                pltpu.SemaphoreType.DMA,
                pltpu.SemaphoreType.DMA((groups // ng,)),
                pltpu.SemaphoreType.DMA((groups,)),
            ],
            compiler_params=pltpu.CompilerParams(
                collective_id=0, has_side_effects=True, vmem_limit_bytes=58 * 2**20
            ),
            cost_estimate=pl.CostEstimate(
                flops=8 * rows * rows * depth, bytes_accessed=28 * 2**20, transcendentals=0
            ),
        )(block_index, pair_density, coulomb[None, :])

    placed = (P(None, "trans", "gvec"), P("gvec"), P("rows"))
    return jax.shard_map(
        body,
        mesh=mesh,
        in_specs=placed,
        out_specs=(P(None, ("rows", "gvec"), "trans"), P(None, "trans", "rows")),
        check_vma=False,
    )
```

```python
import functools

import jax
import jax.numpy as jnp
from jax import lax
from jax.experimental import pallas as pl
from jax.experimental.pallas import tpu as pltpu
from jax.sharding import PartitionSpec as P

MESH = pl.DeviceIdType.MESH
CHUNK = 16
GROUP = 128
PART = 64
HOP = 2
OTHER = 6
SETTLE = 3
TILE = 256
AHEAD = 6


def contract(left, right):
    return lax.dot_general(
        left, right, (((1,), (1,)), ((), ())), preferred_element_type=jnp.float32
    )


def kernel(
    n, ng, index_ref, pd_in, coulomb_ref, rows_out, mirror_out,
    pd_ref, rows_ref, mirror_ref, near, up, down, final, other, weighted, weighted_other, term, arrived,
    near_send, near_recv, share_send, share_recv, up_send, up_recv,
    down_send, down_recv, cross_send, cross_recv, term_send, term_recv,
    load_sem, rows_sem, mirror_sem,
):
    r, t, y = lax.axis_index("rows"), lax.axis_index("trans"), lax.axis_index("gvec")
    line = n // 2
    z, x = t // 2, t % 2
    chunks = near.shape[0]
    half = chunks * CHUNK
    groups = term.shape[0]
    depth = pd_ref.shape[2]
    per = GROUP // CHUNK
    tiles = pd_ref.shape[1] // TILE
    across = {"trans": 2 * z + 1 - x}
    above, below = {"trans": t + 2}, {"trans": t - 2}
    sibling = {"rows": 1 - r}
    load = pltpu.make_async_copy(pd_in, pd_ref, load_sem)
    load.start()

    barrier = pltpu.get_barrier_semaphore()

    def greet(device):
        pl.semaphore_signal(barrier, inc=1, device_id=device, device_id_type=MESH)

    greet(across)
    greet(sibling)
    for p in range(1, ng):
        greet({"gvec": (y + p) % ng})

    @pl.when(z > 0)
    def _():
        greet(below)

    @pl.when(z < line - 1)
    def _():
        greet(above)

    pl.semaphore_wait(
        barrier, 1 + ng + jnp.where(z > 0, 1, 0) + jnp.where(z < line - 1, 1, 0)
    )

    def remote(source, target, send, recv, device):
        return pltpu.make_async_remote_copy(
            src_ref=source, dst_ref=target, send_sem=send, recv_sem=recv,
            device_id=device, device_id_type=MESH,
        )

    def own_rows(side, c):
        return pl.ds(pl.multiple_of(side * half + c * CHUNK, CHUNK), CHUNK)

    def near_copy(c):
        return remote(
            pd_in.at[r, own_rows(1 - x, c), :], near.at[c, r],
            near_send.at[c], near_recv.at[c], across,
        )

    def share_copy(c):
        return remote(near.at[c, r], near.at[c, r], share_send.at[c], share_recv.at[c], sibling)

    def up_copy(c):
        return remote(up.at[c], up.at[c], up_send.at[c], up_recv.at[c], above)

    def down_copy(c):
        return remote(down.at[c], down.at[c], down_send.at[c], down_recv.at[c], below)

    def cross_copy(c):
        return remote(final.at[c], other.at[c], cross_send.at[c], cross_recv.at[c], across)

    def rows_of(i):
        return pl.ds(pl.multiple_of(i * TILE, TILE), TILE)

    def term_copy(g, i, part, p):
        if part is None:
            lanes, slot = pl.ds(0, 2 * GROUP), 0
        else:
            lanes, slot = pl.ds(pl.multiple_of(part * 2 * PART, 2 * PART), 2 * PART), part
        return remote(
            term.at[g, rows_of(i), lanes], arrived.at[p - 1, g, rows_of(i), lanes],
            term_send.at[p - 1, g, i, slot], term_recv.at[p - 1, g, i, slot],
            {"gvec": (y + p) % ng},
        )

    def columns(g):
        return pl.ds(pl.multiple_of(g * GROUP, GROUP), GROUP)

    def mirror_copy(g):
        return pltpu.make_async_copy(
            mirror_ref.at[:, :, columns(g)], mirror_out.at[:, :, columns(g)], mirror_sem.at[g]
        )

    def rows_copy(g):
        return pltpu.make_async_copy(
            rows_ref.at[:, columns(g), :], rows_out.at[:, columns(g), :], rows_sem.at[g]
        )

    source = index_ref[0]
    source_z, source_x = source // 2, source % 2
    here = source_z == z
    mine = source_x == x

    def start_near(c, carry):
        near_copy(c).start()
        return carry

    lax.fori_loop(0, AHEAD, start_near, 0)
    load.wait()
    near_copy(0).wait_recv()
    share_copy(0).start()

    def base(c):
        return jnp.where(mine, pd_ref[:, own_rows(x, c), :], near[c])

    def weigh(held, row, slot, target):
        at = pl.multiple_of((row // PART) * 2 * PART + row % PART, CHUNK)
        scale = coulomb_ref[...]
        real = (held[0].astype(jnp.float32) * scale).astype(jnp.bfloat16)
        imag = (held[1].astype(jnp.float32) * scale).astype(jnp.bfloat16)
        target[slot, pl.ds(at, CHUNK), :depth] = real
        target[slot, pl.ds(at, CHUNK), depth:] = imag
        target[slot, pl.ds(PART + at, CHUNK), :depth] = -imag
        target[slot, pl.ds(PART + at, CHUNK), depth:] = real

    def multiply(i, left):
        total = contract(pd_ref[0, rows_of(i), :], left[:, :depth])
        total = total + contract(pd_ref[1, rows_of(i), :], left[:, depth:])
        return total.astype(jnp.bfloat16)

    share = groups // ng

    def settle(g, i, parts):
        for part in parts:
            for p in range(1, ng):
                term_copy(g, i, part, p).wait_recv()
        at = rows_of(i)
        total = term[g, at, :].astype(jnp.float32)
        for p in range(1, ng):
            total = total + arrived[p - 1, g, at, :].astype(jnp.float32)
        summed = total.astype(jnp.bfloat16)
        real = jnp.concatenate([summed[:, :PART], summed[:, 2 * PART:3 * PART]], axis=1)
        imag = jnp.concatenate([summed[:, PART:2 * PART], summed[:, 3 * PART:]], axis=1)
        mirror_ref[0, at, columns(g)] = real
        mirror_ref[1, at, columns(g)] = -imag

        @pl.when(g // share == y)
        def _():
            rows_ref[0, columns(g % share), at] = real.T
            rows_ref[1, columns(g % share), at] = imag.T

        @pl.when(i == tiles - 1)
        def _():
            mirror_copy(g).start()

            @pl.when(g // share == y)
            def _():
                rows_copy(g % share).start()

    side_groups = groups // 2
    lag = (line - 1) * HOP
    per_part = PART // CHUNK
    pace = per // tiles
    assert per_part == tiles and pace == 2

    def step(s, carry):
        for extra in range(2):
            c = AHEAD + 2 * s + extra

            @pl.when(c < chunks)
            def _(c=c):
                near_copy(c).start()

        @pl.when(s + 1 < chunks)
        def _():
            near_copy(s + 1).wait_recv()
            share_copy(s + 1).start()

        @pl.when(s < chunks)
        def _():
            share_copy(s).wait_recv()

        u = s - z * HOP

        @pl.when((u >= 0) & (u < chunks))
        def _():
            @pl.when(z == 0)
            def _():
                up[u] = base(u)

            @pl.when(z > 0)
            def _():
                up_copy(u).wait_recv()
                up[u] = jnp.where(here, base(u), up[u])

            @pl.when(z < line - 1)
            def _():
                up_copy(u).start()

        d = s - (line - 1 - z) * HOP

        @pl.when((d >= 0) & (d < chunks))
        def _():
            @pl.when(z == line - 1)
            def _():
                down[d] = base(d)

            @pl.when(z < line - 1)
            def _():
                down_copy(d).wait_recv()
                down[d] = jnp.where(here, base(d), down[d])

            @pl.when(z > 0)
            def _():
                down_copy(d).start()

        f = s - lag

        @pl.when((f >= 0) & (f < chunks))
        def _():
            final[f] = jnp.where(source_z <= z, up[f], down[f])
            cross_copy(f).start()
            weigh(final[f], (f % per) * CHUNK, (f // per) % 2, weighted)

        o = f - OTHER

        @pl.when((o >= 0) & (o < chunks))
        def _():
            cross_copy(o).wait_recv()
            weigh(other[o], (o % per_part) * CHUNK, (o // per_part) % 2, weighted_other)

        m = f - per

        @pl.when((m >= 0) & (m < chunks) & (m % pace == 0))
        def _():
            q, i = m // per, (m % per) // pace
            g = x * side_groups + q
            term[g, rows_of(i), :] = multiply(i, weighted.at[q % 2])
            for p in range(1, ng):
                term_copy(g, i, None, p).start()

        m = o - per_part

        @pl.when((m >= 0) & (m < chunks))
        def _():
            q, i = m // per_part, m % per_part
            g = (1 - x) * side_groups + q // 2
            for part in range(2):
                @pl.when(q % 2 == part)
                def _(part=part):
                    term[g, rows_of(i), part * 2 * PART:(part + 1) * 2 * PART] = multiply(
                        i, weighted_other.at[part]
                    )
                    for p in range(1, ng):
                        term_copy(g, i, part, p).start()

        a = f - per - SETTLE

        @pl.when((a >= 0) & (a < chunks) & (a % pace == 0))
        def _():
            settle(x * side_groups + a // per, (a % per) // pace, (None,))

        b = o - per - SETTLE

        @pl.when((b >= 0) & (b < chunks) & (b % per < tiles))
        def _():
            settle((1 - x) * side_groups + b // per, b % per, (0, 1))

        return carry

    lax.fori_loop(0, chunks + lag + OTHER + per + SETTLE, step, 0)

    def drain(c, carry):
        near_copy(c).wait_send()
        share_copy(c).wait_send()
        cross_copy(c).wait_send()

        @pl.when(z < line - 1)
        def _():
            up_copy(c).wait_send()

        @pl.when(z > 0)
        def _():
            down_copy(c).wait_send()

        return carry

    lax.fori_loop(0, chunks, drain, 0)

    def drain_terms(g, carry):
        def drain_tile(i, inner):
            for p in range(1, ng):
                term_copy(x * side_groups + g, i, None, p).wait_send()
                for part in range(2):
                    term_copy((1 - x) * side_groups + g, i, part, p).wait_send()
            return inner

        lax.fori_loop(0, tiles, drain_tile, 0)
        mirror_copy(g).wait()
        mirror_copy(side_groups + g).wait()
        return carry

    lax.fori_loop(0, side_groups, drain_terms, 0)

    def drain_rows(g, carry):
        rows_copy(g).wait()
        return carry

    lax.fori_loop(0, groups // ng, drain_rows, 0)


def solution(mesh):
    n, ng = mesh.shape["trans"], mesh.shape["gvec"]

    def body(pair_density, coulomb, block_index):
        _, rows, depth = pair_density.shape
        chunks = rows // 2 // CHUNK
        groups = rows // GROUP
        slots = pltpu.VMEM((chunks, 2, CHUNK, depth), jnp.bfloat16)
        sems = pltpu.SemaphoreType.DMA((chunks,))
        vmem = pl.BlockSpec(memory_space=pltpu.VMEM)
        hbm = pl.BlockSpec(memory_space=pl.ANY)
        return pl.pallas_call(
            functools.partial(kernel, n, ng),
            out_shape=(
                jax.ShapeDtypeStruct((2, rows // ng, rows), jnp.bfloat16),
                jax.ShapeDtypeStruct((2, rows, rows), jnp.bfloat16),
            ),
            in_specs=[pl.BlockSpec(memory_space=pltpu.SMEM), hbm, vmem],
            out_specs=(hbm, hbm),
            scratch_shapes=[
                pltpu.VMEM(pair_density.shape, jnp.bfloat16),
                pltpu.VMEM((2, rows // ng, rows), jnp.bfloat16),
                pltpu.VMEM((2, rows, rows), jnp.bfloat16),
            ]
            + [slots] * 5
            + [
                pltpu.VMEM((2, 2 * GROUP, 2 * depth), jnp.bfloat16),
                pltpu.VMEM((2, 2 * PART, 2 * depth), jnp.bfloat16),
            ]
            + [
                pltpu.VMEM((groups, rows, 2 * GROUP), jnp.bfloat16),
                pltpu.VMEM((ng - 1, groups, rows, 2 * GROUP), jnp.bfloat16),
            ]
            + [sems] * 10
            + [pltpu.SemaphoreType.DMA((ng - 1, groups, rows // TILE, GROUP // PART))] * 2
            + [
                pltpu.SemaphoreType.DMA,
                pltpu.SemaphoreType.DMA((groups // ng,)),
                pltpu.SemaphoreType.DMA((groups,)),
            ],
            compiler_params=pltpu.CompilerParams(
                collective_id=0, has_side_effects=True, vmem_limit_bytes=58 * 2**20
            ),
            cost_estimate=pl.CostEstimate(
                flops=8 * rows * rows * depth, bytes_accessed=28 * 2**20, transcendentals=0
            ),
        )(block_index, pair_density, coulomb[None, :])

    placed = (P(None, "trans", "gvec"), P("gvec"), P("rows"))
    return jax.shard_map(
        body,
        mesh=mesh,
        in_specs=placed,
        out_specs=(P(None, ("rows", "gvec"), "trans"), P(None, "trans", "rows")),
        check_vma=False,
    )
```

```python
import functools

import jax
import jax.numpy as jnp
from jax import lax
from jax.experimental import pallas as pl
from jax.experimental.pallas import tpu as pltpu
from jax.sharding import PartitionSpec as P

MESH = pl.DeviceIdType.MESH
CHUNK = 16
GROUP = 128
PART = 64
HOP = 4
OTHER = 12
SETTLE = 3
TILE = 256


def contract(left, right):
    return lax.dot_general(
        left, right, (((1,), (1,)), ((), ())), preferred_element_type=jnp.float32
    )


def kernel(
    n, ng, index_ref, pd_in, coulomb_ref, rows_out, mirror_out,
    pd_ref, rows_ref, mirror_ref, near, up, down, final, other, weighted, weighted_other, term, arrived,
    near_send, near_recv, share_send, share_recv, up_send, up_recv,
    down_send, down_recv, cross_send, cross_recv, term_send, term_recv,
    load_sem, rows_sem, mirror_sem,
):
    r, t, y = lax.axis_index("rows"), lax.axis_index("trans"), lax.axis_index("gvec")
    line = n // 2
    z, x = t // 2, t % 2
    chunks = near.shape[0]
    half = chunks * CHUNK
    groups = term.shape[0]
    depth = pd_ref.shape[2]
    per = GROUP // CHUNK
    tiles = pd_ref.shape[1] // TILE
    across = {"trans": 2 * z + 1 - x}
    above, below = {"trans": t + 2}, {"trans": t - 2}
    sibling = {"rows": 1 - r}
    load = pltpu.make_async_copy(pd_in, pd_ref, load_sem)
    load.start()

    barrier = pltpu.get_barrier_semaphore()

    def greet(device):
        pl.semaphore_signal(barrier, inc=1, device_id=device, device_id_type=MESH)

    greet(across)
    greet(sibling)
    for p in range(1, ng):
        greet({"gvec": (y + p) % ng})

    @pl.when(z > 0)
    def _():
        greet(below)

    @pl.when(z < line - 1)
    def _():
        greet(above)

    pl.semaphore_wait(
        barrier, 1 + ng + jnp.where(z > 0, 1, 0) + jnp.where(z < line - 1, 1, 0)
    )

    def remote(source, target, send, recv, device):
        return pltpu.make_async_remote_copy(
            src_ref=source, dst_ref=target, send_sem=send, recv_sem=recv,
            device_id=device, device_id_type=MESH,
        )

    def own_rows(side, c):
        return pl.ds(pl.multiple_of(side * half + c * CHUNK, CHUNK), CHUNK)

    def near_copy(c):
        return remote(
            pd_in.at[r, own_rows(1 - x, c), :], near.at[c, r],
            near_send.at[c], near_recv.at[c], across,
        )

    def share_copy(c):
        return remote(near.at[c, r], near.at[c, r], share_send.at[c], share_recv.at[c], sibling)

    def up_copy(c):
        return remote(up.at[c], up.at[c], up_send.at[c], up_recv.at[c], above)

    def down_copy(c):
        return remote(down.at[c], down.at[c], down_send.at[c], down_recv.at[c], below)

    def cross_copy(c):
        return remote(final.at[c], other.at[c], cross_send.at[c], cross_recv.at[c], across)

    def rows_of(i):
        return pl.ds(pl.multiple_of(i * TILE, TILE), TILE)

    def term_copy(g, i, part, p):
        if part is None:
            lanes, slot = pl.ds(0, 2 * GROUP), 0
        else:
            lanes, slot = pl.ds(pl.multiple_of(part * 2 * PART, 2 * PART), 2 * PART), part
        return remote(
            term.at[g, rows_of(i), lanes], arrived.at[p - 1, g, rows_of(i), lanes],
            term_send.at[p - 1, g, i, slot], term_recv.at[p - 1, g, i, slot],
            {"gvec": (y + p) % ng},
        )

    def columns(g):
        return pl.ds(pl.multiple_of(g * GROUP, GROUP), GROUP)

    def mirror_copy(g):
        return pltpu.make_async_copy(
            mirror_ref.at[:, :, columns(g)], mirror_out.at[:, :, columns(g)], mirror_sem.at[g]
        )

    def rows_copy(g):
        return pltpu.make_async_copy(
            rows_ref.at[:, columns(g), :], rows_out.at[:, columns(g), :], rows_sem.at[g]
        )

    source = index_ref[0]
    source_z, source_x = source // 2, source % 2
    here = source_z == z
    mine = source_x == x

    def start_near(c, carry):
        near_copy(c).start()
        return carry

    lax.fori_loop(0, chunks, start_near, 0)
    load.wait()
    near_copy(0).wait_recv()
    share_copy(0).start()

    def base(c):
        return jnp.where(mine, pd_ref[:, own_rows(x, c), :], near[c])

    def weigh(held, row, slot, target):
        at = pl.multiple_of((row // PART) * 2 * PART + row % PART, CHUNK)
        scale = coulomb_ref[...]
        real = (held[0].astype(jnp.float32) * scale).astype(jnp.bfloat16)
        imag = (held[1].astype(jnp.float32) * scale).astype(jnp.bfloat16)
        target[slot, pl.ds(at, CHUNK), :depth] = real
        target[slot, pl.ds(at, CHUNK), depth:] = imag
        target[slot, pl.ds(PART + at, CHUNK), :depth] = -imag
        target[slot, pl.ds(PART + at, CHUNK), depth:] = real

    def multiply(i, left):
        total = contract(pd_ref[0, rows_of(i), :], left[:, :depth])
        total = total + contract(pd_ref[1, rows_of(i), :], left[:, depth:])
        return total.astype(jnp.bfloat16)

    share = groups // ng

    def settle(g, i, parts):
        for part in parts:
            for p in range(1, ng):
                term_copy(g, i, part, p).wait_recv()
        at = rows_of(i)
        total = term[g, at, :].astype(jnp.float32)
        for p in range(1, ng):
            total = total + arrived[p - 1, g, at, :].astype(jnp.float32)
        summed = total.astype(jnp.bfloat16)
        real = jnp.concatenate([summed[:, :PART], summed[:, 2 * PART:3 * PART]], axis=1)
        imag = jnp.concatenate([summed[:, PART:2 * PART], summed[:, 3 * PART:]], axis=1)
        mirror_ref[0, at, columns(g)] = real
        mirror_ref[1, at, columns(g)] = -imag

        @pl.when(g // share == y)
        def _():
            rows_ref[0, columns(g % share), at] = real.T
            rows_ref[1, columns(g % share), at] = imag.T

        @pl.when(i == tiles - 1)
        def _():
            mirror_copy(g).start()

            @pl.when(g // share == y)
            def _():
                rows_copy(g % share).start()

    side_groups = groups // 2
    lag = (line - 1) * HOP
    per_part = PART // CHUNK
    pace = per // tiles
    assert per_part == tiles and pace == 2

    def step(s, carry):
        @pl.when(s + 1 < chunks)
        def _():
            near_copy(s + 1).wait_recv()
            share_copy(s + 1).start()

        @pl.when(s < chunks)
        def _():
            share_copy(s).wait_recv()

        u = s - z * HOP

        @pl.when((u >= 0) & (u < chunks))
        def _():
            @pl.when(z == 0)
            def _():
                up[u] = base(u)

            @pl.when(z > 0)
            def _():
                up_copy(u).wait_recv()
                up[u] = jnp.where(here, base(u), up[u])

            @pl.when(z < line - 1)
            def _():
                up_copy(u).start()

        d = s - (line - 1 - z) * HOP

        @pl.when((d >= 0) & (d < chunks))
        def _():
            @pl.when(z == line - 1)
            def _():
                down[d] = base(d)

            @pl.when(z < line - 1)
            def _():
                down_copy(d).wait_recv()
                down[d] = jnp.where(here, base(d), down[d])

            @pl.when(z > 0)
            def _():
                down_copy(d).start()

        f = s - lag

        @pl.when((f >= 0) & (f < chunks))
        def _():
            final[f] = jnp.where(source_z <= z, up[f], down[f])
            cross_copy(f).start()
            weigh(final[f], (f % per) * CHUNK, (f // per) % 2, weighted)

        o = f - OTHER

        @pl.when((o >= 0) & (o < chunks))
        def _():
            cross_copy(o).wait_recv()
            weigh(other[o], (o % per_part) * CHUNK, (o // per_part) % 2, weighted_other)

        m = f - per

        @pl.when((m >= 0) & (m < chunks) & (m % pace == 0))
        def _():
            q, i = m // per, (m % per) // pace
            g = x * side_groups + q
            term[g, rows_of(i), :] = multiply(i, weighted.at[q % 2])
            for p in range(1, ng):
                term_copy(g, i, None, p).start()

        m = o - per_part

        @pl.when((m >= 0) & (m < chunks))
        def _():
            q, i = m // per_part, m % per_part
            g = (1 - x) * side_groups + q // 2
            for part in range(2):
                @pl.when(q % 2 == part)
                def _(part=part):
                    term[g, rows_of(i), part * 2 * PART:(part + 1) * 2 * PART] = multiply(
                        i, weighted_other.at[part]
                    )
                    for p in range(1, ng):
                        term_copy(g, i, part, p).start()

        a = f - per - SETTLE

        @pl.when((a >= 0) & (a < chunks) & (a % pace == 0))
        def _():
            settle(x * side_groups + a // per, (a % per) // pace, (None,))

        b = o - per - SETTLE

        @pl.when((b >= 0) & (b < chunks) & (b % per < tiles))
        def _():
            settle((1 - x) * side_groups + b // per, b % per, (0, 1))

        return carry

    lax.fori_loop(0, chunks + lag + OTHER + per + SETTLE, step, 0)

    def drain(c, carry):
        near_copy(c).wait_send()
        share_copy(c).wait_send()
        cross_copy(c).wait_send()

        @pl.when(z < line - 1)
        def _():
            up_copy(c).wait_send()

        @pl.when(z > 0)
        def _():
            down_copy(c).wait_send()

        return carry

    lax.fori_loop(0, chunks, drain, 0)

    def drain_terms(g, carry):
        def drain_tile(i, inner):
            for p in range(1, ng):
                term_copy(x * side_groups + g, i, None, p).wait_send()
                for part in range(2):
                    term_copy((1 - x) * side_groups + g, i, part, p).wait_send()
            return inner

        lax.fori_loop(0, tiles, drain_tile, 0)
        mirror_copy(g).wait()
        mirror_copy(side_groups + g).wait()
        return carry

    lax.fori_loop(0, side_groups, drain_terms, 0)

    def drain_rows(g, carry):
        rows_copy(g).wait()
        return carry

    lax.fori_loop(0, groups // ng, drain_rows, 0)


def solution(mesh):
    n, ng = mesh.shape["trans"], mesh.shape["gvec"]

    def body(pair_density, coulomb, block_index):
        _, rows, depth = pair_density.shape
        chunks = rows // 2 // CHUNK
        groups = rows // GROUP
        slots = pltpu.VMEM((chunks, 2, CHUNK, depth), jnp.bfloat16)
        sems = pltpu.SemaphoreType.DMA((chunks,))
        vmem = pl.BlockSpec(memory_space=pltpu.VMEM)
        hbm = pl.BlockSpec(memory_space=pl.ANY)
        return pl.pallas_call(
            functools.partial(kernel, n, ng),
            out_shape=(
                jax.ShapeDtypeStruct((2, rows // ng, rows), jnp.bfloat16),
                jax.ShapeDtypeStruct((2, rows, rows), jnp.bfloat16),
            ),
            in_specs=[pl.BlockSpec(memory_space=pltpu.SMEM), hbm, vmem],
            out_specs=(hbm, hbm),
            scratch_shapes=[
                pltpu.VMEM(pair_density.shape, jnp.bfloat16),
                pltpu.VMEM((2, rows // ng, rows), jnp.bfloat16),
                pltpu.VMEM((2, rows, rows), jnp.bfloat16),
            ]
            + [slots] * 5
            + [
                pltpu.VMEM((2, 2 * GROUP, 2 * depth), jnp.bfloat16),
                pltpu.VMEM((2, 2 * PART, 2 * depth), jnp.bfloat16),
            ]
            + [
                pltpu.VMEM((groups, rows, 2 * GROUP), jnp.bfloat16),
                pltpu.VMEM((ng - 1, groups, rows, 2 * GROUP), jnp.bfloat16),
            ]
            + [sems] * 10
            + [pltpu.SemaphoreType.DMA((ng - 1, groups, rows // TILE, GROUP // PART))] * 2
            + [
                pltpu.SemaphoreType.DMA,
                pltpu.SemaphoreType.DMA((groups // ng,)),
                pltpu.SemaphoreType.DMA((groups,)),
            ],
            compiler_params=pltpu.CompilerParams(
                collective_id=0, has_side_effects=True, vmem_limit_bytes=58 * 2**20
            ),
            cost_estimate=pl.CostEstimate(
                flops=8 * rows * rows * depth, bytes_accessed=28 * 2**20, transcendentals=0
            ),
        )(block_index, pair_density, coulomb[None, :])

    placed = (P(None, "trans", "gvec"), P("gvec"), P("rows"))
    return jax.shard_map(
        body,
        mesh=mesh,
        in_specs=placed,
        out_specs=(P(None, ("rows", "gvec"), "trans"), P(None, "trans", "rows")),
        check_vma=False,
    )
```

```python
import functools

import jax
import jax.numpy as jnp
from jax import lax
from jax.experimental import pallas as pl
from jax.experimental.pallas import tpu as pltpu
from jax.sharding import PartitionSpec as P

MESH = pl.DeviceIdType.MESH
CHUNK = 16
GROUP = 128
PART = 64
HOP = 2
OTHER = 8
SETTLE = 3
TILE = 256


def contract(left, right):
    return lax.dot_general(
        left, right, (((1,), (1,)), ((), ())), preferred_element_type=jnp.float32
    )


def kernel(
    n, ng, index_ref, pd_in, coulomb_ref, rows_out, mirror_out,
    pd_ref, rows_ref, mirror_ref, near, up, down, final, other, weighted, weighted_other, term, arrived,
    near_send, near_recv, share_send, share_recv, up_send, up_recv,
    down_send, down_recv, cross_send, cross_recv, term_send, term_recv,
    load_sem, rows_sem, mirror_sem,
):
    r, t, y = lax.axis_index("rows"), lax.axis_index("trans"), lax.axis_index("gvec")
    line = n // 2
    z, x = t // 2, t % 2
    chunks = near.shape[0]
    half = chunks * CHUNK
    groups = term.shape[0]
    depth = pd_ref.shape[2]
    per = GROUP // CHUNK
    tiles = pd_ref.shape[1] // TILE
    across = {"trans": 2 * z + 1 - x}
    above, below = {"trans": t + 2}, {"trans": t - 2}
    sibling = {"rows": 1 - r}
    load = pltpu.make_async_copy(pd_in, pd_ref, load_sem)
    load.start()

    barrier = pltpu.get_barrier_semaphore()

    def greet(device):
        pl.semaphore_signal(barrier, inc=1, device_id=device, device_id_type=MESH)

    greet(across)
    greet(sibling)
    for p in range(1, ng):
        greet({"gvec": (y + p) % ng})

    @pl.when(z > 0)
    def _():
        greet(below)

    @pl.when(z < line - 1)
    def _():
        greet(above)

    pl.semaphore_wait(
        barrier, 1 + ng + jnp.where(z > 0, 1, 0) + jnp.where(z < line - 1, 1, 0)
    )

    def remote(source, target, send, recv, device):
        return pltpu.make_async_remote_copy(
            src_ref=source, dst_ref=target, send_sem=send, recv_sem=recv,
            device_id=device, device_id_type=MESH,
        )

    def own_rows(side, c):
        return pl.ds(pl.multiple_of(side * half + c * CHUNK, CHUNK), CHUNK)

    def near_copy(c):
        return remote(
            pd_in.at[r, own_rows(1 - x, c), :], near.at[c, r],
            near_send.at[c], near_recv.at[c], across,
        )

    def share_copy(c):
        return remote(near.at[c, r], near.at[c, r], share_send.at[c], share_recv.at[c], sibling)

    def up_copy(c):
        return remote(up.at[c], up.at[c], up_send.at[c], up_recv.at[c], above)

    def down_copy(c):
        return remote(down.at[c], down.at[c], down_send.at[c], down_recv.at[c], below)

    def cross_copy(c):
        return remote(final.at[c], other.at[c], cross_send.at[c], cross_recv.at[c], across)

    def rows_of(i):
        return pl.ds(pl.multiple_of(i * TILE, TILE), TILE)

    def term_copy(g, i, part, p):
        if part is None:
            lanes, slot = pl.ds(0, 2 * GROUP), 0
        else:
            lanes, slot = pl.ds(pl.multiple_of(part * 2 * PART, 2 * PART), 2 * PART), part
        return remote(
            term.at[g, rows_of(i), lanes], arrived.at[p - 1, g, rows_of(i), lanes],
            term_send.at[p - 1, g, i, slot], term_recv.at[p - 1, g, i, slot],
            {"gvec": (y + p) % ng},
        )

    def columns(g):
        return pl.ds(pl.multiple_of(g * GROUP, GROUP), GROUP)

    def mirror_copy(g):
        return pltpu.make_async_copy(
            mirror_ref.at[:, :, columns(g)], mirror_out.at[:, :, columns(g)], mirror_sem.at[g]
        )

    def rows_copy(g):
        return pltpu.make_async_copy(
            rows_ref.at[:, columns(g), :], rows_out.at[:, columns(g), :], rows_sem.at[g]
        )

    source = index_ref[0]
    source_z, source_x = source // 2, source % 2
    here = source_z == z
    mine = source_x == x

    def start_near(c, carry):
        near_copy(c).start()
        return carry

    lax.fori_loop(0, chunks, start_near, 0)
    load.wait()
    near_copy(0).wait_recv()
    share_copy(0).start()

    def base(c):
        return jnp.where(mine, pd_ref[:, own_rows(x, c), :], near[c])

    def weigh(held, row, slot, target):
        at = pl.multiple_of((row // PART) * 2 * PART + row % PART, CHUNK)
        scale = coulomb_ref[...]
        real = (held[0].astype(jnp.float32) * scale).astype(jnp.bfloat16)
        imag = (held[1].astype(jnp.float32) * scale).astype(jnp.bfloat16)
        target[slot, pl.ds(at, CHUNK), :depth] = real
        target[slot, pl.ds(at, CHUNK), depth:] = imag
        target[slot, pl.ds(PART + at, CHUNK), :depth] = -imag
        target[slot, pl.ds(PART + at, CHUNK), depth:] = real

    def multiply(i, left):
        total = contract(pd_ref[0, rows_of(i), :], left[:, :depth])
        total = total + contract(pd_ref[1, rows_of(i), :], left[:, depth:])
        return total.astype(jnp.bfloat16)

    share = groups // ng

    def settle(g, i, parts):
        for part in parts:
            for p in range(1, ng):
                term_copy(g, i, part, p).wait_recv()
        at = rows_of(i)
        total = term[g, at, :].astype(jnp.float32)
        for p in range(1, ng):
            total = total + arrived[p - 1, g, at, :].astype(jnp.float32)
        summed = total.astype(jnp.bfloat16)
        real = jnp.concatenate([summed[:, :PART], summed[:, 2 * PART:3 * PART]], axis=1)
        imag = jnp.concatenate([summed[:, PART:2 * PART], summed[:, 3 * PART:]], axis=1)
        mirror_ref[0, at, columns(g)] = real
        mirror_ref[1, at, columns(g)] = -imag

        @pl.when(g // share == y)
        def _():
            rows_ref[0, columns(g % share), at] = real.T
            rows_ref[1, columns(g % share), at] = imag.T

        @pl.when(i == tiles - 1)
        def _():
            mirror_copy(g).start()

            @pl.when(g // share == y)
            def _():
                rows_copy(g % share).start()

    side_groups = groups // 2
    lag = (line - 1) * HOP
    per_part = PART // CHUNK
    pace = per // tiles
    assert per_part == tiles and pace == 2

    def step(s, carry):
        @pl.when(s + 1 < chunks)
        def _():
            near_copy(s + 1).wait_recv()
            share_copy(s + 1).start()

        @pl.when(s < chunks)
        def _():
            share_copy(s).wait_recv()

        u = s - z * HOP

        @pl.when((u >= 0) & (u < chunks))
        def _():
            @pl.when(z == 0)
            def _():
                up[u] = base(u)

            @pl.when(z > 0)
            def _():
                up_copy(u).wait_recv()
                up[u] = jnp.where(here, base(u), up[u])

            @pl.when(z < line - 1)
            def _():
                up_copy(u).start()

        d = s - (line - 1 - z) * HOP

        @pl.when((d >= 0) & (d < chunks))
        def _():
            @pl.when(z == line - 1)
            def _():
                down[d] = base(d)

            @pl.when(z < line - 1)
            def _():
                down_copy(d).wait_recv()
                down[d] = jnp.where(here, base(d), down[d])

            @pl.when(z > 0)
            def _():
                down_copy(d).start()

        f = s - lag

        @pl.when((f >= 0) & (f < chunks))
        def _():
            final[f] = jnp.where(source_z <= z, up[f], down[f])
            cross_copy(f).start()
            weigh(final[f], (f % per) * CHUNK, (f // per) % 2, weighted)

        o = f - OTHER

        @pl.when((o >= 0) & (o < chunks))
        def _():
            cross_copy(o).wait_recv()
            weigh(other[o], (o % per_part) * CHUNK, (o // per_part) % 2, weighted_other)

        m = f - per

        @pl.when((m >= 0) & (m < chunks) & (m % pace == 0))
        def _():
            q, i = m // per, (m % per) // pace
            g = x * side_groups + q
            term[g, rows_of(i), :] = multiply(i, weighted.at[q % 2])
            for p in range(1, ng):
                term_copy(g, i, None, p).start()

        m = o - per_part

        @pl.when((m >= 0) & (m < chunks))
        def _():
            q, i = m // per_part, m % per_part
            g = (1 - x) * side_groups + q // 2
            for part in range(2):
                @pl.when(q % 2 == part)
                def _(part=part):
                    term[g, rows_of(i), part * 2 * PART:(part + 1) * 2 * PART] = multiply(
                        i, weighted_other.at[part]
                    )
                    for p in range(1, ng):
                        term_copy(g, i, part, p).start()

        a = f - per - SETTLE

        @pl.when((a >= 0) & (a < chunks) & (a % pace == 0))
        def _():
            settle(x * side_groups + a // per, (a % per) // pace, (None,))

        b = o - per - SETTLE

        @pl.when((b >= 0) & (b < chunks) & (b % per < tiles))
        def _():
            settle((1 - x) * side_groups + b // per, b % per, (0, 1))

        return carry

    lax.fori_loop(0, chunks + lag + OTHER + per + SETTLE, step, 0)

    def drain(c, carry):
        near_copy(c).wait_send()
        share_copy(c).wait_send()
        cross_copy(c).wait_send()

        @pl.when(z < line - 1)
        def _():
            up_copy(c).wait_send()

        @pl.when(z > 0)
        def _():
            down_copy(c).wait_send()

        return carry

    lax.fori_loop(0, chunks, drain, 0)

    def drain_terms(g, carry):
        def drain_tile(i, inner):
            for p in range(1, ng):
                term_copy(x * side_groups + g, i, None, p).wait_send()
                for part in range(2):
                    term_copy((1 - x) * side_groups + g, i, part, p).wait_send()
            return inner

        lax.fori_loop(0, tiles, drain_tile, 0)
        mirror_copy(g).wait()
        mirror_copy(side_groups + g).wait()
        return carry

    lax.fori_loop(0, side_groups, drain_terms, 0)

    def drain_rows(g, carry):
        rows_copy(g).wait()
        return carry

    lax.fori_loop(0, groups // ng, drain_rows, 0)


def solution(mesh):
    n, ng = mesh.shape["trans"], mesh.shape["gvec"]

    def body(pair_density, coulomb, block_index):
        _, rows, depth = pair_density.shape
        chunks = rows // 2 // CHUNK
        groups = rows // GROUP
        slots = pltpu.VMEM((chunks, 2, CHUNK, depth), jnp.bfloat16)
        sems = pltpu.SemaphoreType.DMA((chunks,))
        vmem = pl.BlockSpec(memory_space=pltpu.VMEM)
        hbm = pl.BlockSpec(memory_space=pl.ANY)
        return pl.pallas_call(
            functools.partial(kernel, n, ng),
            out_shape=(
                jax.ShapeDtypeStruct((2, rows // ng, rows), jnp.bfloat16),
                jax.ShapeDtypeStruct((2, rows, rows), jnp.bfloat16),
            ),
            in_specs=[pl.BlockSpec(memory_space=pltpu.SMEM), hbm, vmem],
            out_specs=(hbm, hbm),
            scratch_shapes=[
                pltpu.VMEM(pair_density.shape, jnp.bfloat16),
                pltpu.VMEM((2, rows // ng, rows), jnp.bfloat16),
                pltpu.VMEM((2, rows, rows), jnp.bfloat16),
            ]
            + [slots] * 5
            + [
                pltpu.VMEM((2, 2 * GROUP, 2 * depth), jnp.bfloat16),
                pltpu.VMEM((2, 2 * PART, 2 * depth), jnp.bfloat16),
            ]
            + [
                pltpu.VMEM((groups, rows, 2 * GROUP), jnp.bfloat16),
                pltpu.VMEM((ng - 1, groups, rows, 2 * GROUP), jnp.bfloat16),
            ]
            + [sems] * 10
            + [pltpu.SemaphoreType.DMA((ng - 1, groups, rows // TILE, GROUP // PART))] * 2
            + [
                pltpu.SemaphoreType.DMA,
                pltpu.SemaphoreType.DMA((groups // ng,)),
                pltpu.SemaphoreType.DMA((groups,)),
            ],
            compiler_params=pltpu.CompilerParams(
                collective_id=0, has_side_effects=True, vmem_limit_bytes=58 * 2**20
            ),
            cost_estimate=pl.CostEstimate(
                flops=8 * rows * rows * depth, bytes_accessed=28 * 2**20, transcendentals=0
            ),
        )(block_index, pair_density, coulomb[None, :])

    placed = (P(None, "trans", "gvec"), P("gvec"), P("rows"))
    return jax.shard_map(
        body,
        mesh=mesh,
        in_specs=placed,
        out_specs=(P(None, ("rows", "gvec"), "trans"), P(None, "trans", "rows")),
        check_vma=False,
    )
```
